512 devices in a mesh: seq: 64 (over y, z_lo, core), head: 8 (over z_hi, x).
Axes of the slice: x: 4, y: 8, z: 8 (z_hi: 2, z_lo: 4; z = z_hi * 4 + z_lo), core: 2. Of those that a mesh axis runs over, the one named last changes fastest.
Arguments:
- query: bfloat16 [16384, 3072], P('seq', 'head'), may hold values from -19.25 to 19.25
- key_proj: bfloat16 [16384, 3072], P('seq', 'head'), may hold values from -3.203125 to 3.203125
- value: bfloat16 [16384, 3072], P('seq', 'head'), may hold values from -6 to 6
- head_class: int32 [24], P('head'), may hold values from 0 to 1, as said below
- sink_frame: int32 [1], replicated, may hold values from 0 to 7
- out_weight: bfloat16 [3072, 5120], P('head', 'seq'), may hold values from -0.109375 to 0.109375
Outputs:
- projected: bfloat16 [16384, 5120], P('seq', 'head')
The draws below stay inside these ranges and needn't reach their ends.
Inputs may be any that keep to these rules, and one draw needn't show every extreme that they name: `head_class`: both classes occur among the 24 heads.
All inputs are finite; a program needn't handle non-finite values.
Results may differ from the reference program's by a relative error of at most 0.015.
Values may be sent and summed in bfloat16 or wider, within the bound.
No kernel may reach another device: no remote copies, remote signals or barrier semaphores. Data moves between devices by JAX's collectives and lax.ppermute only.
A program may use at most 64 MiB of HBM per device.

```python
import jax
import jax.numpy as jnp
from jax import lax

D = 5120
HEADS = 24
HD = 128
FRAME_TOK = 2048
FRAMES = 8
TILE = 4
SPLIT = 8
TOK_DEV = 256
TOKENS = 16384
N_HEAD = 8


def draw_key_proj(key, part):
    shape = (TOKENS, HEADS * HD)
    key = jax.random.fold_in(key, 3)
    base = jnp.clip(jax.random.normal(key, shape, jnp.float32), -3.2, 3.2)
    return base.astype(jnp.bfloat16)


def draw_query(key, part):
    shape = (TOKENS, HEADS * HD)
    key = jax.random.fold_in(key, 5)
    result = jnp.clip(jax.random.normal(key, shape, jnp.float32), -4.0, 4.0)
    return result.astype(jnp.bfloat16)


def draw_head_class(key, part):
    key = jax.random.fold_in(key, 11)
    first, second = jax.random.split(key)
    count = jax.random.randint(first, (), 1, HEADS)
    order = jax.random.permutation(second, HEADS)
    return (order < count).astype(jnp.int32)


def levels(own_key, dims, shards, least, high):
    loudness = 1.0
    for dim, shards_of in shards:
        heights = jax.random.uniform(jax.random.fold_in(jax.random.fold_in(own_key, 6), dim), (shards_of,), jnp.float32, least / len(shards), high / len(shards))
        loudness = loudness * jnp.repeat(jnp.exp(heights), dims[dim] // shards_of).reshape((-1,) + (1,) * (len(dims) - 1 - dim))
    return loudness


def centred(key, extent, width, limit, cuts=(), kind=jnp.bfloat16):
    loudness = levels(key, extent, cuts, -0.22, 0.18) if cuts else 1.0
    array = jax.random.normal(key, extent, jnp.float32) * width * loudness
    return jnp.minimum(jnp.maximum(array, -limit), limit).astype(kind)


def setup_inputs(seed: int = 0) -> dict:
    key_list = jax.random.split(jax.random.key(seed), 7)
    query = draw_query(jax.random.fold_in(key_list[6], 71), 0)
    key_proj = draw_key_proj(jax.random.fold_in(key_list[6], 71), 0)
    value = centred(key_list[2], (TOKENS, HEADS * HD), 1.0, 6.0, ((0, 64), (1, 8)))
    head_class = draw_head_class(jax.random.fold_in(key_list[6], 71), 0)
    sink_frame = jax.random.randint(key_list[4], (1,), 0, FRAMES).astype(jnp.int32)
    out_weight = centred(key_list[5], (HEADS * HD, D), (HEADS * HD) ** -0.5, 0.109375, ((0, 8), (1, 64)))
    return {"query": query, "key_proj": key_proj, "value": value, "head_class": head_class, "sink_frame": sink_frame, "out_weight": out_weight}


def attend_sink(query_matrix, key_matrix, value_matrix, sink_k, sink_v):
    score_scale = HD ** -0.5
    scores_main = jnp.dot(query_matrix, key_matrix.T, preferred_element_type=jnp.float32) * score_scale
    scores_sink = jnp.dot(query_matrix, sink_k.T, preferred_element_type=jnp.float32) * score_scale
    largest = jnp.maximum(jnp.max(scores_main, axis=-1), jnp.max(scores_sink, axis=-1))[:, None]
    weights_main = jnp.exp(scores_main - largest)
    weights_sink = jnp.exp(scores_sink - largest)
    totals = jnp.sum(weights_main, axis=-1) + jnp.sum(weights_sink, axis=-1)
    weight_totals = jnp.dot(weights_main.astype(jnp.bfloat16), value_matrix, preferred_element_type=jnp.float32)
    weight_totals = weight_totals + jnp.dot(weights_sink.astype(jnp.bfloat16), sink_v, preferred_element_type=jnp.float32)
    return (weight_totals / totals[:, None]).astype(jnp.bfloat16)


def attend_plain(query_matrix, key_matrix, value_matrix):
    score_scale = HD ** -0.5
    logit_scores = jnp.einsum("yzt,yjt->yzj", query_matrix.astype(jnp.float32), key_matrix.astype(jnp.float32)) * score_scale
    largest = jnp.max(logit_scores, axis=-1)[..., None]
    softmax_weights = jnp.exp(logit_scores - largest)
    totals = jnp.sum(softmax_weights, axis=-1)
    rounded_bfloat = lax.optimization_barrier(softmax_weights.astype(jnp.bfloat16)).astype(jnp.float32)
    weight_totals = jnp.einsum("iut,ito->iuo", rounded_bfloat, value_matrix.astype(jnp.float32))
    return (weight_totals / totals[..., None]).astype(jnp.bfloat16)


def reference(query, key_proj, value, head_class, sink_frame, out_weight):
    sink_index = sink_frame[0].astype(jnp.int32)
    block_count = FRAME_TOK // TILE

    def to_frames(x):
        return x.reshape(SPLIT, FRAMES, TOK_DEV, HD).transpose(1, 0, 2, 3).reshape(FRAMES, FRAME_TOK, HD)

    def from_frames(x):
        return x.reshape(FRAMES, SPLIT, TOK_DEV, HD).transpose(1, 0, 2, 3).reshape(TOKENS, HD)

    def to_tiles(x):
        return x.reshape(FRAMES, block_count, TILE, HD).transpose(1, 0, 2, 3).reshape(block_count, FRAMES * TILE, HD)

    def one_head(items):
        query_matrix, key_matrix, value_matrix, kind = items
        q_frames = to_frames(query_matrix)
        k_frames = to_frames(key_matrix)
        v_frames = to_frames(value_matrix)
        sink_k = lax.dynamic_index_in_dim(k_frames, sink_index, 0, keepdims=False)
        sink_v = lax.dynamic_index_in_dim(v_frames, sink_index, 0, keepdims=False)

        def one_frame(inner):
            q_rows, k_rows, v_rows = inner
            return attend_sink(q_rows, k_rows, v_rows, sink_k, sink_v)

        spatial = lax.map(one_frame, (q_frames, k_frames, v_frames))
        temporal = attend_plain(to_tiles(q_frames), to_tiles(k_frames), to_tiles(v_frames))
        temporal = temporal.reshape(block_count, FRAMES, TILE, HD).transpose(1, 0, 2, 3).reshape(FRAMES, FRAME_TOK, HD)
        return from_frames(jnp.where(kind == 1, temporal, spatial))

    def by_heads(x):
        return x.reshape(TOKENS, HEADS, HD).transpose(1, 0, 2)

    attended = lax.map(one_head, (by_heads(query), by_heads(key_proj), by_heads(value), head_class))
    attended = attended.transpose(1, 0, 2).reshape(TOKENS, HEADS * HD)
    group_width = (HEADS // N_HEAD) * HD
    weight_totals = jnp.zeros((TOKENS, D), jnp.float32)
    for group in range(N_HEAD):
        partial_sum = jnp.dot(attended[:, group * group_width:(group + 1) * group_width], out_weight[group * group_width:(group + 1) * group_width], preferred_element_type=jnp.float32)
        rounded_bfloat = lax.optimization_barrier(partial_sum.astype(jnp.bfloat16))
        weight_totals = weight_totals + rounded_bfloat.astype(jnp.float32)
    return weight_totals.astype(jnp.bfloat16)
```

```python
import functools

import jax
import jax.numpy as jnp
from jax import lax
from jax.experimental import pallas as pl
from jax.experimental.pallas import tpu as pltpu
from jax.sharding import Mesh, PartitionSpec as P

HD = 128
NH = 3
TILE = 4
LOG2E = 1.4426950408889634
SCALE2 = HD**-0.5 * LOG2E
NT = (((1,), (1,)), ((), ()))
TN = (((0,), (0,)), ((), ()))
NN = (((1,), (0,)), ((), ()))


def dot(a, b, dims):
    return lax.dot_general(a, b, dims, preferred_element_type=jnp.float32)


def swap(x, axis):
    return lax.ppermute(x, axis, [(0, 1), (1, 0)])


def spatial_kernel(hc_ref, q_ref, k_ref, v_ref, ko_ref, vo_ref, sa_ref, sb_ref, core_ref, out_ref):
    parts = q_ref.shape[0]
    rows = q_ref.shape[1]
    core = core_ref[0]
    for h in range(NH):
        cols = slice(h * HD, (h + 1) * HD)

        @pl.when(hc_ref[h] == 0)
        def _():
            mine, other = sa_ref[:, cols], sb_ref[:, cols]
            first = core == 0
            sk = jnp.where(first, mine, other)
            sv = jnp.where(first, other, mine)
            keys = jnp.concatenate([k_ref[:, cols], ko_ref[:, cols], sk], axis=0)
            vals = jnp.concatenate([v_ref[:, cols], vo_ref[:, cols], sv], axis=0)
            for p in range(parts):
                q = q_ref[p, :, cols]
                s = dot(keys, q, NT) * SCALE2
                m = jnp.max(s, axis=0, keepdims=True)
                w = jnp.exp2(s - m)
                total = jnp.sum(w, axis=0, keepdims=True)
                o = dot(vals, w.astype(jnp.bfloat16), TN)
                out_ref[p, cols, :] = (o / total).astype(jnp.bfloat16)
                lse = m + jnp.log2(total)
                hi = lse.astype(jnp.bfloat16).astype(jnp.float32)
                mid = (lse - hi).astype(jnp.bfloat16).astype(jnp.float32)
                low = lse - hi - mid
                row = lax.broadcasted_iota(jnp.int32, (16, rows), 0)
                stats = jnp.where(row == 0, hi, jnp.where(row == 1, mid, low))
                out_ref[p, NH * HD + 16 * h : NH * HD + 16 * h + 16, :] = stats.astype(jnp.bfloat16)


def spatial(hc, q, k, v, ko, vo, sa, sb, core):
    parts, rows, width = q.shape
    smem = pl.BlockSpec(memory_space=pltpu.SMEM)
    vmem = pl.BlockSpec(memory_space=pltpu.VMEM)
    return pl.pallas_call(
        spatial_kernel,
        out_shape=jax.ShapeDtypeStruct((parts, width + 16 * NH, rows), jnp.bfloat16),
        in_specs=[smem] + [vmem] * 7 + [smem],
        out_specs=vmem,
        compiler_params=pltpu.CompilerParams(vmem_limit_bytes=24 * 1024 * 1024),
        name="spatial",
    )(hc, q, k, v, ko, vo, sa, sb, core)


def temporal_kernel(hc_ref, q_ref, k_ref, v_ref, out_ref):
    rows = q_ref.shape[0]
    span = rows // 8
    for h in range(NH):
        cols = slice(h * HD, (h + 1) * HD)

        @pl.when(hc_ref[h] == 1)
        def _():
            s = dot(q_ref[:, cols], k_ref[:, cols], NT) * SCALE2
            i = lax.broadcasted_iota(jnp.int32, (rows, rows), 0)
            j = lax.broadcasted_iota(jnp.int32, (rows, rows), 1)
            s = jnp.where((i % span) // TILE == (j % span) // TILE, s, -jnp.inf)
            w = jnp.exp2(s - jnp.max(s, axis=1, keepdims=True))
            total = jnp.sum(w, axis=1, keepdims=True)
            o = dot(w.astype(jnp.bfloat16), v_ref[:, cols], NN)
            out_ref[:, cols] = (o / total).astype(jnp.bfloat16)


def temporal(hc, q, k, v):
    smem = pl.BlockSpec(memory_space=pltpu.SMEM)
    vmem = pl.BlockSpec(memory_space=pltpu.VMEM)
    return pl.pallas_call(
        temporal_kernel,
        out_shape=jax.ShapeDtypeStruct(q.shape, jnp.bfloat16),
        in_specs=[smem] + [vmem] * 3,
        out_specs=vmem,
        compiler_params=pltpu.CompilerParams(vmem_limit_bytes=16 * 1024 * 1024),
        name="temporal",
    )(hc, q, k, v)


def combine_kernel(hc_ref, part_ref, back_ref, out_ref):
    parts = part_ref.shape[0]
    for h in range(NH):
        cols = slice(h * HD, (h + 1) * HD)

        @pl.when(hc_ref[h] == 0)
        def _():
            lses = []
            for p in range(parts):
                st = part_ref[p, NH * HD + 16 * h : NH * HD + 16 * h + 16, :].astype(jnp.float32)
                lses.append(st[0:1] + st[1:2] + st[2:3])
            m = functools.reduce(jnp.maximum, lses)
            es = [jnp.exp2(l - m) for l in lses]
            inv = 1.0 / sum(es)
            o = sum(part_ref[p, cols, :].astype(jnp.float32) * (es[p] * inv) for p in range(parts))
            out_ref[:, cols] = o.T.astype(jnp.bfloat16)

        @pl.when(hc_ref[h] != 0)
        def _():
            out_ref[:, cols] = back_ref[:, cols]


def combine(hc, part, back):
    smem = pl.BlockSpec(memory_space=pltpu.SMEM)
    vmem = pl.BlockSpec(memory_space=pltpu.VMEM)
    return pl.pallas_call(
        combine_kernel,
        out_shape=jax.ShapeDtypeStruct(back.shape, jnp.bfloat16),
        in_specs=[smem, vmem, vmem],
        out_specs=vmem,
        compiler_params=pltpu.CompilerParams(vmem_limit_bytes=16 * 1024 * 1024),
        name="combine",
    )(hc, part, back)


def project_kernel(w_ref, own_ref, other_ref, weight_ref, out_ref):
    here = w_ref[0] * 4
    there = 4 - here
    total = jnp.zeros(out_ref.shape, jnp.float32)
    for i in range(4):
        total += dot(own_ref[i], weight_ref[here + i], NT)
        total += dot(other_ref[i], weight_ref[there + i], NT)
    out_ref[...] = total.astype(jnp.bfloat16)


def project(w, own, other, weight):
    smem = pl.BlockSpec(memory_space=pltpu.SMEM)
    vmem = pl.BlockSpec(memory_space=pltpu.VMEM)
    return pl.pallas_call(
        project_kernel,
        out_shape=jax.ShapeDtypeStruct((own.shape[1], weight.shape[1]), jnp.bfloat16),
        in_specs=[smem, vmem, vmem, vmem],
        out_specs=vmem,
        compiler_params=pltpu.CompilerParams(vmem_limit_bytes=24 * 1024 * 1024),
        name="project",
    )(w, own, other, weight)


def to_all(x, axis):
    n = lax.axis_size(axis)
    return lax.all_to_all(jnp.broadcast_to(x[None], (n,) + x.shape), axis, 0, 0, tiled=True)


def per_device(query, key_proj, value, head_class, sink_frame, out_weight):
    rows, width = query.shape
    core = lax.axis_index("c")
    sink = sink_frame[0]
    is_temporal = jnp.repeat(head_class == 1, HD)

    turned = lax.ppermute(
        out_weight.T, ("a", "b", "w", "x"), [(y * 8 + h, h * 8 + y) for y in range(8) for h in range(8)]
    )
    weight = lax.all_gather(turned, ("z", "c"), axis=0, tiled=True)
    weight = lax.all_gather(weight, ("a", "b"), axis=0)

    key_value = jnp.concatenate([key_proj, value], axis=0)
    other_kv = swap(key_value, "b")
    group_query = to_all(query, "a")

    carried = jnp.where(core == 0, key_proj, value)
    given = swap(jnp.where(core == 0, value, key_proj), "c")
    candidate = jnp.where(sink % 2 == core, carried, given)
    pieces = [x.reshape(4, rows // 4, width) for x in (query, key_proj, value)]
    pieces = jnp.concatenate(pieces + [jnp.zeros_like(pieces[0])], axis=1)
    sent = jnp.where(is_temporal, pieces, candidate[None])
    got = lax.all_to_all(sent, "z", 0, 0, tiled=True)

    sink_part = lax.dynamic_index_in_dim(got, sink // 2, 0, keepdims=False)
    sink_pair = jnp.concatenate([sink_part, swap(sink_part, "b")], axis=0)
    sink_other = swap(sink_pair, "c")

    half = rows // 8
    tokens = got.reshape(4, 4, 2, half, width)[:, :3]
    keep = jnp.where(core == 0, tokens[:, :, 0], tokens[:, :, 1])
    give = jnp.where(core == 0, tokens[:, :, 1], tokens[:, :, 0])
    come = swap(give, "c")
    first = jnp.where(core == 0, keep, come)
    second = jnp.where(core == 0, come, keep)
    both = jnp.stack([first, second], axis=1)
    tq, tk, tv = (both[:, :, i].reshape(rows, width) for i in range(3))
    back = temporal(head_class, tq, tk, tv)
    back = lax.all_to_all(back.reshape(8, half, width), ("z", "c"), 0, 0, tiled=True).reshape(rows, width)

    part = spatial(
        head_class, group_query, key_proj, value, other_kv[:rows], other_kv[rows:], sink_pair, sink_other,
        core.reshape(1),
    )
    part = lax.all_to_all(part, "a", 0, 0, tiled=True)
    attended = combine(head_class, part, back)

    other = swap(attended, "w")
    own_all = to_all(attended, "x")
    other_all = to_all(other, "x")
    return project(lax.axis_index("w").reshape(1), own_all, other_all, weight)


def solution(mesh):
    fine = Mesh(mesh.devices.reshape(4, 2, 4, 2, 2, 4), ("a", "b", "z", "c", "w", "x"))
    seq, head = ("a", "b", "z", "c"), ("w", "x")
    in_specs = (P(seq, head), P(seq, head), P(seq, head), P(head), P(), P(head, seq))
    return jax.shard_map(per_device, mesh=fine, in_specs=in_specs, out_specs=P(seq, head), check_vma=False)
```

```python
import functools

import jax
import jax.numpy as jnp
from jax import lax
from jax.experimental import pallas as pl
from jax.experimental.pallas import tpu as pltpu
from jax.sharding import Mesh, PartitionSpec as P

HD = 128
NH = 3
TILE = 4
LOG2E = 1.4426950408889634
SCALE2 = HD**-0.5 * LOG2E
NT = (((1,), (1,)), ((), ()))
TN = (((0,), (0,)), ((), ()))
NN = (((1,), (0,)), ((), ()))


def dot(a, b, dims):
    return lax.dot_general(a, b, dims, preferred_element_type=jnp.float32)


def swap(x, axis):
    return lax.ppermute(x, axis, [(0, 1), (1, 0)])


def spatial_kernel(hc_ref, core_ref, at_ref, k_ref, v_ref, okv_ref, sa_ref, sb_ref, q_ref, *rest):
    count = len(rest) - 1
    out_refs, stats_ref = rest[:count], rest[-1]
    rows = k_ref.shape[0]
    first = core_ref[0] == 0
    for h in range(NH):
        cols = slice(h * HD, (h + 1) * HD)

        @pl.when(hc_ref[h] == 0)
        def _():
            mine, other = sa_ref[:, cols], sb_ref[:, cols]
            sk = jnp.where(first, mine, other)
            sv = jnp.where(first, other, mine)
            keys = jnp.concatenate([k_ref[:, cols], okv_ref[:rows, cols], sk], axis=0)
            vals = jnp.concatenate([v_ref[:, cols], okv_ref[rows:, cols], sv], axis=0)
            for i in range(count):
                at = at_ref[i] if q_ref.shape[0] > 1 else 0
                s = dot(keys, q_ref[at, :rows, cols], NT) * SCALE2
                m = jnp.max(s, axis=0, keepdims=True)
                w = jnp.exp2(s - m)
                total = jnp.sum(w, axis=0, keepdims=True)
                o = dot(vals, w.astype(jnp.bfloat16), TN)
                out_refs[i][cols, :] = (o / total).astype(jnp.bfloat16)
                lse = m + jnp.log2(total)
                hi = lse.astype(jnp.bfloat16).astype(jnp.float32)
                mid = (lse - hi).astype(jnp.bfloat16).astype(jnp.float32)
                stats_ref[i, 3 * h : 3 * h + 1, :] = hi
                stats_ref[i, 3 * h + 1 : 3 * h + 2, :] = mid
                stats_ref[i, 3 * h + 2 : 3 * h + 3, :] = lse - hi - mid

    for i in range(count):
        out_refs[i][NH * HD :, :] = stats_ref[i].astype(jnp.bfloat16)


def spatial(hc, core, at, k, v, okv, sa, sb, queries, after=()):
    rows, width = k.shape
    smem = pl.BlockSpec(memory_space=pltpu.SMEM)
    vmem = pl.BlockSpec(memory_space=pltpu.VMEM)
    count = at.shape[0]
    shape = jax.ShapeDtypeStruct((width + 16, rows), jnp.bfloat16)

    def body(*refs):
        spatial_kernel(*refs[:9], *refs[9 + len(after) :])

    return pl.pallas_call(
        body,
        out_shape=[shape] * count,
        in_specs=[smem] * 3 + [vmem] * 6 + [pl.BlockSpec(memory_space=pl.ANY)] * len(after),
        out_specs=[vmem] * count,
        scratch_shapes=[pltpu.VMEM((count, 16, rows), jnp.float32)],
        compiler_params=pltpu.CompilerParams(vmem_limit_bytes=16 * 1024 * 1024),
        name="spatial",
    )(hc, core, at, k, v, okv, sa, sb, queries, *after)


def temporal_kernel(hc_ref, q_ref, k_ref, v_ref, out_ref):
    rows = q_ref.shape[0]
    span = rows // 8
    for h in range(NH):
        cols = slice(h * HD, (h + 1) * HD)

        @pl.when(hc_ref[h] == 1)
        def _():
            s = dot(q_ref[:, cols], k_ref[:, cols], NT) * SCALE2
            i = lax.broadcasted_iota(jnp.int32, (rows, rows), 0)
            j = lax.broadcasted_iota(jnp.int32, (rows, rows), 1)
            s = jnp.where((i % span) // TILE == (j % span) // TILE, s, -jnp.inf)
            w = jnp.exp2(s - jnp.max(s, axis=1, keepdims=True))
            total = jnp.sum(w, axis=1, keepdims=True)
            o = dot(w.astype(jnp.bfloat16), v_ref[:, cols], NN)
            out_ref[:, cols] = (o / total).astype(jnp.bfloat16)


def temporal(hc, q, k, v):
    smem = pl.BlockSpec(memory_space=pltpu.SMEM)
    vmem = pl.BlockSpec(memory_space=pltpu.VMEM)
    return pl.pallas_call(
        temporal_kernel,
        out_shape=jax.ShapeDtypeStruct(q.shape, jnp.bfloat16),
        in_specs=[smem] + [vmem] * 3,
        out_specs=vmem,
        compiler_params=pltpu.CompilerParams(vmem_limit_bytes=16 * 1024 * 1024),
        name="temporal",
    )(hc, q, k, v)


def combine_kernel(hc_ref, p0_ref, p1_ref, p2_ref, p3_ref, back_ref, out_ref):
    parts = (p0_ref, p1_ref, p2_ref, p3_ref)
    stats = [p[NH * HD :, :].astype(jnp.float32) for p in parts]
    for h in range(NH):
        cols = slice(h * HD, (h + 1) * HD)

        @pl.when(hc_ref[h] == 0)
        def _():
            lses = [st[3 * h : 3 * h + 1] + st[3 * h + 1 : 3 * h + 2] + st[3 * h + 2 : 3 * h + 3] for st in stats]
            m = functools.reduce(jnp.maximum, lses)
            es = [jnp.exp2(l - m) for l in lses]
            inv = 1.0 / sum(es)
            o = sum(p[cols, :].astype(jnp.float32) * (e * inv) for p, e in zip(parts, es))
            out_ref[:, cols] = o.T.astype(jnp.bfloat16)

        @pl.when(hc_ref[h] != 0)
        def _():
            out_ref[:, cols] = back_ref[:, cols]


def combine(hc, parts, back):
    smem = pl.BlockSpec(memory_space=pltpu.SMEM)
    vmem = pl.BlockSpec(memory_space=pltpu.VMEM)
    return pl.pallas_call(
        combine_kernel,
        out_shape=jax.ShapeDtypeStruct(back.shape, jnp.bfloat16),
        in_specs=[smem] + [vmem] * 5,
        out_specs=vmem,
        compiler_params=pltpu.CompilerParams(vmem_limit_bytes=16 * 1024 * 1024),
        name="combine",
    )(hc, *parts, back)


def project_kernel(group_ref, a0_ref, a1_ref, a2_ref, a3_ref, weight_ref, *rest):
    total = rest[0][...] if len(rest) == 2 else None
    for i, ref in enumerate((a0_ref, a1_ref, a2_ref, a3_ref)):
        rows = jnp.concatenate([weight_ref[j, group_ref[i]] for j in range(weight_ref.shape[0])], axis=0)
        term = dot(ref[...], rows, NT)
        total = term if total is None else total + term
    rest[-1][...] = total.astype(rest[-1].dtype)


def project(groups, attended, weight, begin=None):
    rows, columns = attended[0].shape[0], weight.shape[0] * weight.shape[2]
    smem = pl.BlockSpec(memory_space=pltpu.SMEM)
    vmem = pl.BlockSpec(memory_space=pltpu.VMEM)
    inputs = [*attended, weight] + ([] if begin is None else [begin])
    return pl.pallas_call(
        project_kernel,
        out_shape=jax.ShapeDtypeStruct((rows, columns), jnp.float32 if begin is None else jnp.bfloat16),
        in_specs=[smem] + [vmem] * len(inputs),
        out_specs=vmem,
        compiler_params=pltpu.CompilerParams(vmem_limit_bytes=16 * 1024 * 1024),
        name="project",
    )(groups, *inputs)


def shifted(x, axis, by):
    n = lax.axis_size(axis)
    return lax.ppermute(x, axis, [(i, (i + by) % n) for i in range(n)])


def mirrored(x, by, back=False):
    pairs = [(y, (y + (by if y % 2 == 0 else -by)) % 8) for y in range(8)]
    return lax.ppermute(x, ("a", "b"), [(d, s) for s, d in pairs] if back else pairs)


def after(x, *others):
    return lax.optimization_barrier((x,) + others)[0]


def per_device(query, key_proj, value, head_class, sink_frame, out_weight):
    rows, width = query.shape
    core = lax.axis_index("c")
    sink = sink_frame[0]
    is_temporal = jnp.repeat(head_class == 1, HD)

    carried = jnp.where(core == 0, key_proj, value)
    given = swap(jnp.where(core == 0, value, key_proj), "c")
    candidate = jnp.where(sink % 2 == core, carried, given)
    pieces = [x.reshape(4, rows // 4, width) for x in (query, key_proj, value)]
    pieces = jnp.concatenate(pieces + [jnp.zeros_like(pieces[0])], axis=1)
    sent = jnp.where(is_temporal, pieces, candidate[None])
    got = lax.all_to_all(sent, "z", 0, 0, tiled=True)

    other_kv = swap(jnp.concatenate([key_proj, value], axis=0), "b")
    moves = (-3, 2, -1)
    y = 2 * lax.axis_index("a") + lax.axis_index("b")
    side = jnp.where(y % 2 == 0, -1, 1)
    chosen = jnp.stack([(y + side * abs(by)) % 8 for by in moves] + [y])

    turned = lax.ppermute(
        out_weight.T, ("a", "b", "w", "x"), [(y * 8 + h, h * 8 + y) for y in range(8) for h in range(8)]
    )
    early, other_kv = lax.optimization_barrier((query, other_kv))
    gathered = lax.all_gather(jnp.concatenate([early, turned], axis=0), ("a", "b"), axis=0)

    sink_part = lax.dynamic_index_in_dim(got, sink // 2, 0, keepdims=False)
    sink_pair = jnp.concatenate([sink_part, swap(sink_part, "b")], axis=0)
    sink_other = swap(sink_pair, "c")

    half = rows // 8
    tokens = got.reshape(4, 4, 2, half, width)[:, :3]
    keep = jnp.where(core == 0, tokens[:, :, 0], tokens[:, :, 1])
    give = jnp.where(core == 0, tokens[:, :, 1], tokens[:, :, 0])
    come = swap(give, "c")
    first = jnp.where(core == 0, keep, come)
    second = jnp.where(core == 0, come, keep)
    both = jnp.stack([first, second], axis=1)
    tq, tk, tv = (both[:, :, i].reshape(rows, width) for i in range(3))
    back = temporal(head_class, tq, tk, tv)
    gathered, back = lax.optimization_barrier((gathered, sink_other, back))[::2]
    weight = lax.all_gather(gathered[:, rows:], ("z", "c"), axis=0)
    back = lax.all_to_all(back.reshape(8, half, width), ("z", "c"), 0, 0, tiled=True).reshape(rows, width)

    keys = (key_proj, value, other_kv, sink_pair, sink_other)
    away = spatial(head_class, core.reshape(1), chosen[:3], *keys, gathered)
    (here,) = spatial(head_class, core.reshape(1), chosen[3:], *keys, query[None], after=away[:1])
    parts = [mirrored(x, by, back=True) for x, by in zip(away, moves)]
    attended = combine(head_class, [*parts, here], back)

    other = swap(attended, "w")
    x, w = lax.axis_index("x"), lax.axis_index("w")
    own_all = [attended] + [shifted(attended, "x", by) for by in (1, 2, 3)]
    other_all = [other] + [shifted(other, "x", by) for by in (1, 2, 3)]
    groups = (x - jnp.arange(4)) % 4
    begin = project(groups + 4 * w, own_all, weight)
    return project(groups + 4 * (1 - w), other_all, weight, begin)


def solution(mesh):
    fine = Mesh(mesh.devices.reshape(4, 2, 4, 2, 2, 4), ("a", "b", "z", "c", "w", "x"))
    seq, head = ("a", "b", "z", "c"), ("w", "x")
    in_specs = (P(seq, head), P(seq, head), P(seq, head), P(head), P(), P(head, seq))
    return jax.shard_map(per_device, mesh=fine, in_specs=in_specs, out_specs=P(seq, head), check_vma=False)
```

```python
import functools

import jax
import jax.numpy as jnp
from jax import lax
from jax.experimental import pallas as pl
from jax.experimental.pallas import tpu as pltpu
from jax.sharding import Mesh, PartitionSpec as P

HD = 128
NH = 3
TILE = 4
LOG2E = 1.4426950408889634
SCALE2 = HD**-0.5 * LOG2E
NT = (((1,), (1,)), ((), ()))
TN = (((0,), (0,)), ((), ()))
NN = (((1,), (0,)), ((), ()))


def dot(a, b, dims):
    return lax.dot_general(a, b, dims, preferred_element_type=jnp.float32)


def swap(x, axis):
    return lax.ppermute(x, axis, [(0, 1), (1, 0)])


def spatial_kernel(hc_ref, core_ref, k_ref, v_ref, okv_ref, sa_ref, sb_ref, *rest):
    count = len(rest) // 2
    q_refs, out_refs, stats_ref = rest[:count], rest[count:-1], rest[-1]
    rows = k_ref.shape[0]
    first = core_ref[0] == 0
    for h in range(NH):
        cols = slice(h * HD, (h + 1) * HD)

        @pl.when(hc_ref[h] == 0)
        def _():
            mine, other = sa_ref[:, cols], sb_ref[:, cols]
            sk = jnp.where(first, mine, other)
            sv = jnp.where(first, other, mine)
            keys = jnp.concatenate([k_ref[:, cols], okv_ref[:rows, cols], sk], axis=0)
            vals = jnp.concatenate([v_ref[:, cols], okv_ref[rows:, cols], sv], axis=0)
            for i in range(count):
                s = dot(keys, q_refs[i][:, cols], NT) * SCALE2
                m = jnp.max(s, axis=0, keepdims=True)
                w = jnp.exp2(s - m)
                total = jnp.sum(w, axis=0, keepdims=True)
                o = dot(vals, w.astype(jnp.bfloat16), TN)
                out_refs[i][cols, :] = (o / total).astype(jnp.bfloat16)
                lse = m + jnp.log2(total)
                hi = lse.astype(jnp.bfloat16).astype(jnp.float32)
                mid = (lse - hi).astype(jnp.bfloat16).astype(jnp.float32)
                stats_ref[i, 3 * h : 3 * h + 1, :] = hi
                stats_ref[i, 3 * h + 1 : 3 * h + 2, :] = mid
                stats_ref[i, 3 * h + 2 : 3 * h + 3, :] = lse - hi - mid

    for i in range(count):
        out_refs[i][NH * HD :, :] = stats_ref[i].astype(jnp.bfloat16)


def spatial(hc, core, k, v, okv, sa, sb, queries, after=()):
    rows, width = k.shape
    smem = pl.BlockSpec(memory_space=pltpu.SMEM)
    vmem = pl.BlockSpec(memory_space=pltpu.VMEM)
    count = len(queries)
    shape = jax.ShapeDtypeStruct((width + 16, rows), jnp.bfloat16)

    def body(*refs):
        spatial_kernel(*refs[: 7 + count], *refs[7 + count + len(after) :])

    return pl.pallas_call(
        body,
        out_shape=[shape] * count,
        in_specs=[smem] * 2 + [vmem] * (5 + count) + [pl.BlockSpec(memory_space=pl.ANY)] * len(after),
        out_specs=[vmem] * count,
        scratch_shapes=[pltpu.VMEM((count, 16, rows), jnp.float32)],
        compiler_params=pltpu.CompilerParams(vmem_limit_bytes=16 * 1024 * 1024),
        name="spatial",
    )(hc, core, k, v, okv, sa, sb, *queries, *after)


def temporal_kernel(hc_ref, q_ref, k_ref, v_ref, out_ref):
    rows = q_ref.shape[0]
    span = rows // 8
    for h in range(NH):
        cols = slice(h * HD, (h + 1) * HD)

        @pl.when(hc_ref[h] == 1)
        def _():
            s = dot(q_ref[:, cols], k_ref[:, cols], NT) * SCALE2
            i = lax.broadcasted_iota(jnp.int32, (rows, rows), 0)
            j = lax.broadcasted_iota(jnp.int32, (rows, rows), 1)
            s = jnp.where((i % span) // TILE == (j % span) // TILE, s, -jnp.inf)
            w = jnp.exp2(s - jnp.max(s, axis=1, keepdims=True))
            total = jnp.sum(w, axis=1, keepdims=True)
            o = dot(w.astype(jnp.bfloat16), v_ref[:, cols], NN)
            out_ref[:, cols] = (o / total).astype(jnp.bfloat16)


def temporal(hc, q, k, v):
    smem = pl.BlockSpec(memory_space=pltpu.SMEM)
    vmem = pl.BlockSpec(memory_space=pltpu.VMEM)
    return pl.pallas_call(
        temporal_kernel,
        out_shape=jax.ShapeDtypeStruct(q.shape, jnp.bfloat16),
        in_specs=[smem] + [vmem] * 3,
        out_specs=vmem,
        compiler_params=pltpu.CompilerParams(vmem_limit_bytes=16 * 1024 * 1024),
        name="temporal",
    )(hc, q, k, v)


def combine_kernel(hc_ref, p0_ref, p1_ref, p2_ref, p3_ref, back_ref, out_ref):
    parts = (p0_ref, p1_ref, p2_ref, p3_ref)
    stats = [p[NH * HD :, :].astype(jnp.float32) for p in parts]
    for h in range(NH):
        cols = slice(h * HD, (h + 1) * HD)

        @pl.when(hc_ref[h] == 0)
        def _():
            lses = [st[3 * h : 3 * h + 1] + st[3 * h + 1 : 3 * h + 2] + st[3 * h + 2 : 3 * h + 3] for st in stats]
            m = functools.reduce(jnp.maximum, lses)
            es = [jnp.exp2(l - m) for l in lses]
            inv = 1.0 / sum(es)
            o = sum(p[cols, :].astype(jnp.float32) * (e * inv) for p, e in zip(parts, es))
            out_ref[:, cols] = o.T.astype(jnp.bfloat16)

        @pl.when(hc_ref[h] != 0)
        def _():
            out_ref[:, cols] = back_ref[:, cols]


def combine(hc, parts, back):
    smem = pl.BlockSpec(memory_space=pltpu.SMEM)
    vmem = pl.BlockSpec(memory_space=pltpu.VMEM)
    return pl.pallas_call(
        combine_kernel,
        out_shape=jax.ShapeDtypeStruct(back.shape, jnp.bfloat16),
        in_specs=[smem] + [vmem] * 5,
        out_specs=vmem,
        compiler_params=pltpu.CompilerParams(vmem_limit_bytes=16 * 1024 * 1024),
        name="combine",
    )(hc, *parts, back)


def project_kernel(at_ref, all_ref, low_ref, high_ref, *rest):
    total = None
    for i, (ref, j) in enumerate(((low_ref, 0), (low_ref, 1), (high_ref, 0), (high_ref, 1))):
        rows = jnp.concatenate([ref[k, j] for k in range(ref.shape[0])], axis=0)
        term = dot(all_ref[i], rows, NT)
        total = term if total is None else total + term
    rest[-1][...] = total.astype(rest[-1].dtype)


def project(at, attended, weight, dtype, after=()):
    count, rows, width = attended.shape
    columns = weight.shape[0] * weight.shape[2]
    block = (weight.shape[0], 2) + weight.shape[2:]
    return pl.pallas_call(
        project_kernel,
        out_shape=jax.ShapeDtypeStruct((rows, columns), dtype),
        grid_spec=pltpu.PrefetchScalarGridSpec(
            num_scalar_prefetch=1,
            grid=(1,),
            in_specs=[
                pl.BlockSpec((count, rows, width), lambda i, at: (0, 0, 0)),
                pl.BlockSpec(block, lambda i, at: (0, at[0], 0, 0)),
                pl.BlockSpec(block, lambda i, at: (0, at[1], 0, 0)),
            ]
            + [pl.BlockSpec(memory_space=pl.ANY)] * len(after),
            out_specs=pl.BlockSpec((rows, columns), lambda i, at: (0, 0)),
        ),
        compiler_params=pltpu.CompilerParams(vmem_limit_bytes=50 * 1024 * 1024),
        name="project",
    )(at, attended, weight, weight, *after)


def shifted(x, axis, by):
    n = lax.axis_size(axis)
    return lax.ppermute(x, axis, [(i, (i + by) % n) for i in range(n)])


def mirrored(x, by):
    return lax.ppermute(x, ("a", "b"), [(y, (y + (by if y % 2 == 0 else -by)) % 8) for y in range(8)])


def after(x, *others):
    return lax.optimization_barrier((x,) + others)[0]


def per_device(query, key_proj, value, head_class, sink_frame, out_weight):
    rows, width = query.shape
    core = lax.axis_index("c")
    sink = sink_frame[0]
    is_temporal = jnp.repeat(head_class == 1, HD)

    turned = lax.ppermute(
        out_weight.T,
        ("a", "b", "x"),
        [((4 * u + v) * 4 + x, (4 * u + x) * 4 + v) for u in range(2) for v in range(4) for x in range(4)],
    )
    given = swap(jnp.where(core == 0, value, key_proj), "c")
    carried = jnp.where(core == 0, key_proj, value)
    candidate = jnp.where(sink % 2 == core, carried, given)
    pieces = [x.reshape(4, rows // 4, width) for x in (query, key_proj, value)]
    pieces = jnp.concatenate(pieces + [jnp.zeros_like(pieces[0])], axis=1)
    sent = jnp.where(is_temporal, pieces, candidate[None])

    sent, turned = lax.optimization_barrier((sent, turned))
    got = lax.all_to_all(sent, "z", 0, 0, tiled=True)
    beside = swap(jnp.concatenate([key_proj, value, turned], axis=0), "b")
    other_kv, beside = beside[: 2 * rows], beside[2 * rows :]
    even = lax.axis_index("b") == 0
    pair = [jnp.where(even, turned, beside), jnp.where(even, beside, turned)]
    moves = (-3, 3, -1)
    moving = jnp.concatenate([query] + pair, axis=0)
    moved = [mirrored(moving, by) for by in moves]

    got, moved = lax.optimization_barrier((got, moved))
    queries = [x[:rows] for x in moved]
    weight = jnp.concatenate(pair + [x[rows:] for x in moved], axis=0).reshape(8, *turned.shape)
    weight = lax.all_gather(weight, ("z", "c"), axis=0)
    sink_part = lax.dynamic_index_in_dim(got, sink // 2, 0, keepdims=False)
    sink_pair = jnp.concatenate([sink_part, swap(sink_part, "b")], axis=0)

    half = rows // 8
    tokens = got.reshape(4, 4, 2, half, width)[:, :3]
    keep = jnp.where(core == 0, tokens[:, :, 0], tokens[:, :, 1])
    give = jnp.where(core == 0, tokens[:, :, 1], tokens[:, :, 0])
    come = swap(give, "c")
    first = jnp.where(core == 0, keep, come)
    second = jnp.where(core == 0, come, keep)
    both = jnp.stack([first, second], axis=1)
    tq, tk, tv = (both[:, :, i].reshape(rows, width) for i in range(3))
    back = temporal(head_class, tq, tk, tv)
    sink_pair, back = lax.optimization_barrier((sink_pair, back))
    sink_other = swap(sink_pair, "c")
    back = lax.all_to_all(back.reshape(8, half, width), ("z", "c"), 0, 0, tiled=True).reshape(rows, width)

    keys = (key_proj, value, other_kv, sink_pair, sink_other)
    away = spatial(head_class, core.reshape(1), *keys, queries)
    (here,) = spatial(head_class, core.reshape(1), *keys, [query], after=away[:1])
    parts = [mirrored(x, by) for x, by in zip(away, moves)]
    attended = combine(head_class, [*parts, here], back)

    everyone = lax.all_gather(attended, "x", axis=0)
    w = lax.axis_index("w")
    ahead = (2 * jnp.stack([1 - w, w])[:, None] + jnp.arange(2) - lax.axis_index("a")) % 4
    places = jnp.where(ahead == 1, jnp.where(even, 2, 3), jnp.where(ahead == 3, jnp.where(even, 3, 2), ahead // 2))
    theirs = project(places[0], everyone, weight, jnp.bfloat16)
    mine = project(places[1], everyone, weight, jnp.float32, (theirs,))
    return (mine + swap(theirs, "w").astype(jnp.float32)).astype(jnp.bfloat16)


def solution(mesh):
    fine = Mesh(mesh.devices.reshape(4, 2, 4, 2, 2, 4), ("a", "b", "z", "c", "w", "x"))
    seq, head = ("a", "b", "z", "c"), ("w", "x")
    in_specs = (P(seq, head), P(seq, head), P(seq, head), P(head), P(), P(head, seq))
    return jax.shard_map(per_device, mesh=fine, in_specs=in_specs, out_specs=P(seq, head), check_vma=False)
```

```python
import functools

import jax
import jax.numpy as jnp
from jax import lax
from jax.experimental import pallas as pl
from jax.experimental.pallas import tpu as pltpu
from jax.sharding import Mesh, PartitionSpec as P

HD = 128
NH = 3
TILE = 4
LOG2E = 1.4426950408889634
SCALE2 = HD**-0.5 * LOG2E
NT = (((1,), (1,)), ((), ()))
TN = (((0,), (0,)), ((), ()))
NN = (((1,), (0,)), ((), ()))


def dot(a, b, dims):
    return lax.dot_general(a, b, dims, preferred_element_type=jnp.float32)


def swap(x, axis):
    return lax.ppermute(x, axis, [(0, 1), (1, 0)])


def spatial_kernel(hc_ref, core_ref, k_ref, v_ref, okv_ref, sa_ref, sb_ref, *rest):
    count = len(rest) // 2
    q_refs, out_refs, stats_ref = rest[:count], rest[count:-1], rest[-1]
    rows = k_ref.shape[0]
    first = core_ref[0] == 0
    for h in range(NH):
        cols = slice(h * HD, (h + 1) * HD)

        @pl.when(hc_ref[h] == 0)
        def _():
            mine, other = sa_ref[:, cols], sb_ref[:, cols]
            sk = jnp.where(first, mine, other)
            sv = jnp.where(first, other, mine)
            keys = jnp.concatenate([k_ref[:, cols], okv_ref[:rows, cols], sk], axis=0)
            vals = jnp.concatenate([v_ref[:, cols], okv_ref[rows:, cols], sv], axis=0)
            for i in range(count):
                s = dot(keys, q_refs[i][:, cols], NT) * SCALE2
                m = jnp.max(s, axis=0, keepdims=True)
                w = jnp.exp2(s - m)
                total = jnp.sum(w, axis=0, keepdims=True)
                o = dot(vals, w.astype(jnp.bfloat16), TN)
                out_refs[i][cols, :] = (o / total).astype(jnp.bfloat16)
                lse = m + jnp.log2(total)
                hi = lse.astype(jnp.bfloat16).astype(jnp.float32)
                mid = (lse - hi).astype(jnp.bfloat16).astype(jnp.float32)
                stats_ref[i, 3 * h : 3 * h + 1, :] = hi
                stats_ref[i, 3 * h + 1 : 3 * h + 2, :] = mid
                stats_ref[i, 3 * h + 2 : 3 * h + 3, :] = lse - hi - mid

    for i in range(count):
        out_refs[i][NH * HD :, :] = stats_ref[i].astype(jnp.bfloat16)


def spatial(hc, core, k, v, okv, sa, sb, queries, after=()):
    rows, width = k.shape
    smem = pl.BlockSpec(memory_space=pltpu.SMEM)
    vmem = pl.BlockSpec(memory_space=pltpu.VMEM)
    count = len(queries)
    shape = jax.ShapeDtypeStruct((width + 16, rows), jnp.bfloat16)

    def body(*refs):
        spatial_kernel(*refs[: 7 + count], *refs[7 + count + len(after) :])

    return pl.pallas_call(
        body,
        out_shape=[shape] * count,
        in_specs=[smem] * 2 + [vmem] * (5 + count) + [pl.BlockSpec(memory_space=pl.ANY)] * len(after),
        out_specs=[vmem] * count,
        scratch_shapes=[pltpu.VMEM((count, 16, rows), jnp.float32)],
        compiler_params=pltpu.CompilerParams(vmem_limit_bytes=16 * 1024 * 1024),
        name="spatial",
    )(hc, core, k, v, okv, sa, sb, *queries, *after)


def temporal_kernel(hc_ref, q_ref, k_ref, v_ref, out_ref):
    rows = q_ref.shape[0]
    span = rows // 8
    for h in range(NH):
        cols = slice(h * HD, (h + 1) * HD)

        @pl.when(hc_ref[h] == 1)
        def _():
            s = dot(q_ref[:, cols], k_ref[:, cols], NT) * SCALE2
            i = lax.broadcasted_iota(jnp.int32, (rows, rows), 0)
            j = lax.broadcasted_iota(jnp.int32, (rows, rows), 1)
            s = jnp.where((i % span) // TILE == (j % span) // TILE, s, -jnp.inf)
            w = jnp.exp2(s - jnp.max(s, axis=1, keepdims=True))
            total = jnp.sum(w, axis=1, keepdims=True)
            o = dot(w.astype(jnp.bfloat16), v_ref[:, cols], NN)
            out_ref[:, cols] = (o / total).astype(jnp.bfloat16)


def temporal(hc, q, k, v):
    smem = pl.BlockSpec(memory_space=pltpu.SMEM)
    vmem = pl.BlockSpec(memory_space=pltpu.VMEM)
    return pl.pallas_call(
        temporal_kernel,
        out_shape=jax.ShapeDtypeStruct(q.shape, jnp.bfloat16),
        in_specs=[smem] + [vmem] * 3,
        out_specs=vmem,
        compiler_params=pltpu.CompilerParams(vmem_limit_bytes=16 * 1024 * 1024),
        name="temporal",
    )(hc, q, k, v)


def combine_kernel(hc_ref, p0_ref, p1_ref, p2_ref, p3_ref, back_ref, out_ref):
    parts = (p0_ref, p1_ref, p2_ref, p3_ref)
    stats = [p[NH * HD :, :].astype(jnp.float32) for p in parts]
    for h in range(NH):
        cols = slice(h * HD, (h + 1) * HD)

        @pl.when(hc_ref[h] == 0)
        def _():
            lses = [st[3 * h : 3 * h + 1] + st[3 * h + 1 : 3 * h + 2] + st[3 * h + 2 : 3 * h + 3] for st in stats]
            m = functools.reduce(jnp.maximum, lses)
            es = [jnp.exp2(l - m) for l in lses]
            inv = 1.0 / sum(es)
            o = sum(p[cols, :].astype(jnp.float32) * (e * inv) for p, e in zip(parts, es))
            out_ref[:, cols] = o.T.astype(jnp.bfloat16)

        @pl.when(hc_ref[h] != 0)
        def _():
            out_ref[:, cols] = back_ref[:, cols]


def combine(hc, parts, back):
    smem = pl.BlockSpec(memory_space=pltpu.SMEM)
    vmem = pl.BlockSpec(memory_space=pltpu.VMEM)
    return pl.pallas_call(
        combine_kernel,
        out_shape=jax.ShapeDtypeStruct(back.shape, jnp.bfloat16),
        in_specs=[smem] + [vmem] * 5,
        out_specs=vmem,
        compiler_params=pltpu.CompilerParams(vmem_limit_bytes=16 * 1024 * 1024),
        name="combine",
    )(hc, *parts, back)


def project_kernel(at_ref, all_ref, weight_ref, *rest):
    out_ref, total_ref = rest[-2:]
    step = pl.program_id(0)
    total = None
    for i in range(all_ref.shape[0]):
        rows = jnp.concatenate([weight_ref[k, i] for k in range(weight_ref.shape[0])], axis=0)
        term = dot(all_ref[i], rows, NT)
        total = term if total is None else total + term

    @pl.when(step == 0)
    def _():
        total_ref[...] = total

    @pl.when(step == 1)
    def _():
        out_ref[...] = (total_ref[...] + total).astype(out_ref.dtype)


def project(at, attended, weight, dtype, after=()):
    count, rows, width = attended.shape
    columns = weight.shape[0] * weight.shape[2]
    block = (weight.shape[0], 2) + weight.shape[2:]
    return pl.pallas_call(
        project_kernel,
        out_shape=jax.ShapeDtypeStruct((rows, columns), dtype),
        grid_spec=pltpu.PrefetchScalarGridSpec(
            num_scalar_prefetch=1,
            grid=(2,),
            in_specs=[
                pl.BlockSpec((count // 2, rows, width), lambda i, at: (i, 0, 0)),
                pl.BlockSpec(block, lambda i, at: (0, at[i], 0, 0)),
            ]
            + [pl.BlockSpec(memory_space=pl.ANY)] * len(after),
            out_specs=pl.BlockSpec((rows, columns), lambda i, at: (0, 0)),
            scratch_shapes=[pltpu.VMEM((rows, columns), jnp.float32)],
        ),
        compiler_params=pltpu.CompilerParams(vmem_limit_bytes=50 * 1024 * 1024),
        name="project",
    )(at, attended, weight, *after)


def shifted(x, axis, by):
    n = lax.axis_size(axis)
    return lax.ppermute(x, axis, [(i, (i + by) % n) for i in range(n)])


def mirrored(x, by):
    return lax.ppermute(x, ("a", "b"), [(y, (y + (by if y % 2 == 0 else -by)) % 8) for y in range(8)])


def after(x, *others):
    return lax.optimization_barrier((x,) + others)[0]


def per_device(query, key_proj, value, head_class, sink_frame, out_weight):
    rows, width = query.shape
    core = lax.axis_index("c")
    sink = sink_frame[0]
    is_temporal = jnp.repeat(head_class == 1, HD)

    turned = lax.ppermute(
        out_weight.T,
        ("a", "b", "x"),
        [((4 * u + v) * 4 + x, (4 * u + x) * 4 + v) for u in range(2) for v in range(4) for x in range(4)],
    )
    given = swap(jnp.where(core == 0, value, key_proj), "c")
    carried = jnp.where(core == 0, key_proj, value)
    candidate = jnp.where(sink % 2 == core, carried, given)
    pieces = [x.reshape(4, rows // 4, width) for x in (query, key_proj, value)]
    pieces = jnp.concatenate(pieces + [jnp.zeros_like(pieces[0])], axis=1)
    sent = jnp.where(is_temporal, pieces, candidate[None])

    sent, turned = lax.optimization_barrier((sent, turned))
    got = lax.all_to_all(sent, "z", 0, 0, tiled=True)
    beside = swap(jnp.concatenate([key_proj, value, turned], axis=0), "b")
    other_kv, beside = beside[: 2 * rows], beside[2 * rows :]
    even = lax.axis_index("b") == 0
    pair = [jnp.where(even, turned, beside), jnp.where(even, beside, turned)]
    moves = (-3, 3, -1)
    moving = jnp.concatenate([query] + pair, axis=0)
    moved = [mirrored(moving, by) for by in moves]

    got, moved = lax.optimization_barrier((got, moved))
    queries = [x[:rows] for x in moved]
    weight = jnp.concatenate(pair + [x[rows:] for x in moved], axis=0).reshape(8, *turned.shape)
    weight = lax.all_gather(weight, ("z", "c"), axis=0)
    sink_part = lax.dynamic_index_in_dim(got, sink // 2, 0, keepdims=False)
    sink_pair = jnp.concatenate([sink_part, swap(sink_part, "b")], axis=0)

    half = rows // 8
    tokens = got.reshape(4, 4, 2, half, width)[:, :3]
    keep = jnp.where(core == 0, tokens[:, :, 0], tokens[:, :, 1])
    give = jnp.where(core == 0, tokens[:, :, 1], tokens[:, :, 0])
    come = swap(give, "c")
    first = jnp.where(core == 0, keep, come)
    second = jnp.where(core == 0, come, keep)
    both = jnp.stack([first, second], axis=1)
    tq, tk, tv = (both[:, :, i].reshape(rows, width) for i in range(3))
    back = temporal(head_class, tq, tk, tv)
    sink_pair, back = lax.optimization_barrier((sink_pair, back))
    sink_other = swap(sink_pair, "c")
    back = lax.all_to_all(back.reshape(8, half, width), ("z", "c"), 0, 0, tiled=True).reshape(rows, width)

    keys = (key_proj, value, other_kv, sink_pair, sink_other)
    away = spatial(head_class, core.reshape(1), *keys, queries)
    (here,) = spatial(head_class, core.reshape(1), *keys, [query], after=away[:1])
    parts = [mirrored(x, by) for x, by in zip(away, moves)]
    attended = combine(head_class, [*parts, here], back)

    everyone = lax.all_gather(attended, "x", axis=0)
    w = lax.axis_index("w")
    ahead = (2 * jnp.stack([1 - w, w])[:, None] + jnp.arange(2) - lax.axis_index("a")) % 4
    places = jnp.where(ahead == 1, jnp.where(even, 2, 3), jnp.where(ahead == 3, jnp.where(even, 3, 2), ahead // 2))
    theirs = project(places[0], everyone, weight, jnp.bfloat16)
    mine = project(places[1], everyone, weight, jnp.float32, (theirs,))
    return (mine + swap(theirs, "w").astype(jnp.float32)).astype(jnp.bfloat16)


def solution(mesh):
    fine = Mesh(mesh.devices.reshape(4, 2, 4, 2, 2, 4), ("a", "b", "z", "c", "w", "x"))
    seq, head = ("a", "b", "z", "c"), ("w", "x")
    in_specs = (P(seq, head), P(seq, head), P(seq, head), P(head), P(), P(head, seq))
    return jax.shard_map(per_device, mesh=fine, in_specs=in_specs, out_specs=P(seq, head), check_vma=False)
```

```python
import functools

import jax
import jax.numpy as jnp
from jax import lax
from jax.experimental import pallas as pl
from jax.experimental.pallas import tpu as pltpu
from jax.sharding import Mesh, PartitionSpec as P

HD = 128
NH = 3
TILE = 4
LOG2E = 1.4426950408889634
SCALE2 = HD**-0.5 * LOG2E
NT = (((1,), (1,)), ((), ()))
TN = (((0,), (0,)), ((), ()))
NN = (((1,), (0,)), ((), ()))


def dot(a, b, dims):
    return lax.dot_general(a, b, dims, preferred_element_type=jnp.float32)


def swap(x, axis):
    return lax.ppermute(x, axis, [(0, 1), (1, 0)])


def spatial_kernel(hc_ref, core_ref, k_ref, v_ref, okv_ref, sa_ref, sb_ref, *rest):
    count = len(rest) // 2
    q_refs, out_refs, stats_ref = rest[:count], rest[count:-1], rest[-1]
    rows = k_ref.shape[0]
    first = core_ref[0] == 0
    for h in range(NH):
        cols = slice(h * HD, (h + 1) * HD)

        @pl.when(hc_ref[h] == 0)
        def _():
            mine, other = sa_ref[:, cols], sb_ref[:, cols]
            sk = jnp.where(first, mine, other)
            sv = jnp.where(first, other, mine)
            keys = jnp.concatenate([k_ref[:, cols], okv_ref[:rows, cols], sk], axis=0)
            vals = jnp.concatenate([v_ref[:, cols], okv_ref[rows:, cols], sv], axis=0)
            for i in range(count):
                s = dot(keys, q_refs[i][:, cols], NT) * SCALE2
                m = jnp.max(s, axis=0, keepdims=True)
                w = jnp.exp2(s - m)
                total = jnp.sum(w, axis=0, keepdims=True)
                o = dot(vals, w.astype(jnp.bfloat16), TN)
                out_refs[i][cols, :] = (o / total).astype(jnp.bfloat16)
                lse = m + jnp.log2(total)
                hi = lse.astype(jnp.bfloat16).astype(jnp.float32)
                mid = (lse - hi).astype(jnp.bfloat16).astype(jnp.float32)
                stats_ref[i, 3 * h : 3 * h + 1, :] = hi
                stats_ref[i, 3 * h + 1 : 3 * h + 2, :] = mid
                stats_ref[i, 3 * h + 2 : 3 * h + 3, :] = lse - hi - mid

    for i in range(count):
        out_refs[i][NH * HD :, :] = stats_ref[i].astype(jnp.bfloat16)


def spatial(hc, core, k, v, okv, sa, sb, queries, after=()):
    rows, width = k.shape
    smem = pl.BlockSpec(memory_space=pltpu.SMEM)
    vmem = pl.BlockSpec(memory_space=pltpu.VMEM)
    count = len(queries)
    shape = jax.ShapeDtypeStruct((width + 16, rows), jnp.bfloat16)

    def body(*refs):
        spatial_kernel(*refs[: 7 + count], *refs[7 + count + len(after) :])

    return pl.pallas_call(
        body,
        out_shape=[shape] * count,
        in_specs=[smem] * 2 + [vmem] * (5 + count) + [pl.BlockSpec(memory_space=pl.ANY)] * len(after),
        out_specs=[vmem] * count,
        scratch_shapes=[pltpu.VMEM((count, 16, rows), jnp.float32)],
        compiler_params=pltpu.CompilerParams(vmem_limit_bytes=16 * 1024 * 1024),
        name="spatial",
    )(hc, core, k, v, okv, sa, sb, *queries, *after)


def temporal_kernel(hc_ref, q_ref, k_ref, v_ref, out_ref):
    rows = q_ref.shape[0]
    span = rows // 8
    for h in range(NH):
        cols = slice(h * HD, (h + 1) * HD)

        @pl.when(hc_ref[h] == 1)
        def _():
            s = dot(q_ref[:, cols], k_ref[:, cols], NT) * SCALE2
            i = lax.broadcasted_iota(jnp.int32, (rows, rows), 0)
            j = lax.broadcasted_iota(jnp.int32, (rows, rows), 1)
            s = jnp.where((i % span) // TILE == (j % span) // TILE, s, -jnp.inf)
            w = jnp.exp2(s - jnp.max(s, axis=1, keepdims=True))
            total = jnp.sum(w, axis=1, keepdims=True)
            o = dot(w.astype(jnp.bfloat16), v_ref[:, cols], NN)
            out_ref[:, cols] = (o / total).astype(jnp.bfloat16)


def temporal(hc, q, k, v):
    smem = pl.BlockSpec(memory_space=pltpu.SMEM)
    vmem = pl.BlockSpec(memory_space=pltpu.VMEM)
    return pl.pallas_call(
        temporal_kernel,
        out_shape=jax.ShapeDtypeStruct(q.shape, jnp.bfloat16),
        in_specs=[smem] + [vmem] * 3,
        out_specs=vmem,
        compiler_params=pltpu.CompilerParams(vmem_limit_bytes=16 * 1024 * 1024),
        name="temporal",
    )(hc, q, k, v)


def combine_kernel(hc_ref, p0_ref, p1_ref, p2_ref, p3_ref, back_ref, out_ref):
    parts = (p0_ref, p1_ref, p2_ref, p3_ref)
    stats = [p[NH * HD :, :].astype(jnp.float32) for p in parts]
    for h in range(NH):
        cols = slice(h * HD, (h + 1) * HD)

        @pl.when(hc_ref[h] == 0)
        def _():
            lses = [st[3 * h : 3 * h + 1] + st[3 * h + 1 : 3 * h + 2] + st[3 * h + 2 : 3 * h + 3] for st in stats]
            m = functools.reduce(jnp.maximum, lses)
            es = [jnp.exp2(l - m) for l in lses]
            inv = 1.0 / sum(es)
            o = sum(p[cols, :].astype(jnp.float32) * (e * inv) for p, e in zip(parts, es))
            out_ref[:, cols] = o.T.astype(jnp.bfloat16)

        @pl.when(hc_ref[h] != 0)
        def _():
            out_ref[:, cols] = back_ref[:, cols]


def combine(hc, parts, back):
    smem = pl.BlockSpec(memory_space=pltpu.SMEM)
    vmem = pl.BlockSpec(memory_space=pltpu.VMEM)
    return pl.pallas_call(
        combine_kernel,
        out_shape=jax.ShapeDtypeStruct(back.shape, jnp.bfloat16),
        in_specs=[smem] + [vmem] * 5,
        out_specs=vmem,
        compiler_params=pltpu.CompilerParams(vmem_limit_bytes=16 * 1024 * 1024),
        name="combine",
    )(hc, *parts, back)


def project_kernel(at_ref, all_ref, low_ref, high_ref, *rest):
    total = None
    for i, (ref, j) in enumerate(((low_ref, 0), (low_ref, 1), (high_ref, 0), (high_ref, 1))):
        rows = jnp.concatenate([ref[k, j] for k in range(ref.shape[0])], axis=0)
        term = dot(all_ref[i], rows, NT)
        total = term if total is None else total + term
    rest[-1][...] = total.astype(rest[-1].dtype)


def project(at, attended, weight, dtype, after=()):
    count, rows, width = attended.shape
    columns = weight.shape[0] * weight.shape[2]
    block = (weight.shape[0], 2) + weight.shape[2:]
    return pl.pallas_call(
        project_kernel,
        out_shape=jax.ShapeDtypeStruct((rows, columns), dtype),
        grid_spec=pltpu.PrefetchScalarGridSpec(
            num_scalar_prefetch=1,
            grid=(1,),
            in_specs=[
                pl.BlockSpec((count, rows, width), lambda i, at: (0, 0, 0)),
                pl.BlockSpec(block, lambda i, at: (0, at[0], 0, 0)),
                pl.BlockSpec(block, lambda i, at: (0, at[1], 0, 0)),
            ]
            + [pl.BlockSpec(memory_space=pl.ANY)] * len(after),
            out_specs=pl.BlockSpec((rows, columns), lambda i, at: (0, 0)),
        ),
        compiler_params=pltpu.CompilerParams(vmem_limit_bytes=50 * 1024 * 1024),
        name="project",
    )(at, attended, weight, weight, *after)


def shifted(x, axis, by):
    n = lax.axis_size(axis)
    return lax.ppermute(x, axis, [(i, (i + by) % n) for i in range(n)])


def mirrored(x, by):
    return lax.ppermute(x, ("a", "b"), [(y, (y + (by if y % 2 == 0 else -by)) % 8) for y in range(8)])


def after(x, *others):
    return lax.optimization_barrier((x,) + others)[0]


def per_device(query, key_proj, value, head_class, sink_frame, out_weight):
    rows, width = query.shape
    core = lax.axis_index("c")
    sink = sink_frame[0]
    is_temporal = jnp.repeat(head_class == 1, HD)

    turned = lax.ppermute(
        out_weight.T,
        ("a", "b", "x"),
        [((4 * u + v) * 4 + x, (4 * u + x) * 4 + v) for u in range(2) for v in range(4) for x in range(4)],
    )
    given = swap(jnp.where(core == 0, value, key_proj), "c")
    carried = jnp.where(core == 0, key_proj, value)
    candidate = jnp.where(sink % 2 == core, carried, given)
    pieces = [x.reshape(4, rows // 4, width) for x in (query, key_proj, value)]
    pieces = jnp.concatenate(pieces + [jnp.zeros_like(pieces[0])], axis=1)
    sent = jnp.where(is_temporal, pieces, candidate[None])

    sent, turned = lax.optimization_barrier((sent, turned))
    got = lax.all_to_all(sent, "z", 0, 0, tiled=True)
    beside = swap(jnp.concatenate([key_proj, value, turned], axis=0), "b")
    other_kv, beside = beside[: 2 * rows], beside[2 * rows :]
    even = lax.axis_index("b") == 0
    pair = [jnp.where(even, turned, beside), jnp.where(even, beside, turned)]
    moves = (-3, 3, -1)
    moving = jnp.concatenate([query] + pair, axis=0)
    moved = [mirrored(moving, by) for by in moves]

    got, moved = lax.optimization_barrier((got, moved))
    queries = [x[:rows] for x in moved]
    weight = jnp.concatenate(pair + [x[rows:] for x in moved], axis=0).reshape(8, *turned.shape)
    weight = lax.all_gather(weight, ("z", "c"), axis=0)
    sink_part = lax.dynamic_index_in_dim(got, sink // 2, 0, keepdims=False)
    sink_pair = jnp.concatenate([sink_part, swap(sink_part, "b")], axis=0)

    half = rows // 8
    tokens = got.reshape(4, 4, 2, half, width)[:, :3]
    keep = jnp.where(core == 0, tokens[:, :, 0], tokens[:, :, 1])
    give = jnp.where(core == 0, tokens[:, :, 1], tokens[:, :, 0])
    come = swap(give, "c")
    first = jnp.where(core == 0, keep, come)
    second = jnp.where(core == 0, come, keep)
    both = jnp.stack([first, second], axis=1)
    tq, tk, tv = (both[:, :, i].reshape(rows, width) for i in range(3))
    back = temporal(head_class, tq, tk, tv)
    sink_other = swap(sink_pair, "c")
    back = lax.all_to_all(back.reshape(8, half, width), ("z", "c"), 0, 0, tiled=True).reshape(rows, width)

    keys = (key_proj, value, other_kv, sink_pair, sink_other)
    away = spatial(head_class, core.reshape(1), *keys, queries)
    (here,) = spatial(head_class, core.reshape(1), *keys, [query], after=away[:1])
    parts = [mirrored(x, by) for x, by in zip(away, moves)]
    attended = combine(head_class, [*parts, here], back)

    everyone = lax.all_gather(attended, "x", axis=0)
    w = lax.axis_index("w")
    ahead = (2 * jnp.stack([1 - w, w])[:, None] + jnp.arange(2) - lax.axis_index("a")) % 4
    places = jnp.where(ahead == 1, jnp.where(even, 2, 3), jnp.where(ahead == 3, jnp.where(even, 3, 2), ahead // 2))
    theirs = project(places[0], everyone, weight, jnp.bfloat16)
    mine = project(places[1], everyone, weight, jnp.float32, (theirs,))
    return (mine + swap(theirs, "w").astype(jnp.float32)).astype(jnp.bfloat16)


def solution(mesh):
    fine = Mesh(mesh.devices.reshape(4, 2, 4, 2, 2, 4), ("a", "b", "z", "c", "w", "x"))
    seq, head = ("a", "b", "z", "c"), ("w", "x")
    in_specs = (P(seq, head), P(seq, head), P(seq, head), P(head), P(), P(head, seq))
    return jax.shard_map(per_device, mesh=fine, in_specs=in_specs, out_specs=P(seq, head), check_vma=False)
```
